32 devices in a mesh: dp: 4 (over y, x), expert: 4 (over z), wshard: 2 (over core).
Axes of the slice: x: 2, y: 2, z: 4, core: 2. Of those that a mesh axis runs over, the one named last changes fastest.
Arguments:
- tokens: bfloat16 [16384, 768], P(('dp', 'expert', 'wshard')), may hold values from -6 to 6
- cotangent: bfloat16 [16384, 768], P(('dp', 'expert', 'wshard')), may hold values from -6 to 6
- segment_ids: int32 [32, 512], P(('dp', 'expert', 'wshard')), may hold values from 0 to 3, never falling along the last dimension, each value on 1 to 256 neighbouring positions
- routes: int32 [16384, 2], P(('dp', 'expert', 'wshard')), may hold values from 0 to 7, all different within a row; in each aligned block of 512 rows (0 to 511, 512 to 1023, ...) at most 160 rows name the same one
- gain_attn: bfloat16 [768], P('wshard'), may hold values from 0.099609375 to 1.8984375
- gain_ffn: bfloat16 [768], P('wshard'), may hold values from 0.099609375 to 1.8984375
- w_query: bfloat16 [768, 768], P('wshard'), may hold values from -0.21875 to 0.21875
- w_key: bfloat16 [768, 768], P('wshard'), may hold values from -0.21875 to 0.21875
- w_value: bfloat16 [768, 768], P('wshard'), may hold values from -0.21875 to 0.21875
- w_project: bfloat16 [768, 768], P('wshard'), may hold values from -0.875 to 0.875
- router: bfloat16 [768, 8], P('wshard'), may hold values from -0.15625 to 0.15625
- bias_table: bfloat16 [12, 32], P('wshard'), may hold values from -4 to 4
- expert_in: bfloat16 [8, 768, 3072], P(('expert', 'wshard')), may hold values from -0.21875 to 0.21875
- expert_out: bfloat16 [8, 3072, 768], P(('expert', 'wshard')), may hold values from -0.21875 to 0.21875
Outputs:
- mixed: bfloat16 [16384, 768], P(('dp', 'expert', 'wshard'))
- grad_tokens: float32 [16384, 768], P(('dp', 'expert', 'wshard'))
- grad_gain_attn: float32 [768], P('wshard')
- grad_gain_ffn: float32 [768], P('wshard')
- grad_w_query: float32 [768, 768], P('wshard')
- grad_w_key: float32 [768, 768], P('wshard')
- grad_w_value: float32 [768, 768], P('wshard')
- grad_w_project: float32 [768, 768], P('wshard')
- grad_router: float32 [768, 8], P('wshard')
- grad_bias_table: float32 [12, 32], P('wshard')
- grad_expert_in: float32 [8, 768, 3072], P(('expert', 'wshard'), None, 'dp')
- grad_expert_out: float32 [8, 3072, 768], P(('expert', 'wshard'), 'dp')
The draws below stay inside these ranges and needn't reach their ends.
Inputs may be any that keep to these rules, and one draw needn't show every extreme that they name: `routes`: in the rows of one device no expert is named more than 160 times, a bound that some block reaches; the two experts of a token differ. `segment_ids`: ids never fall along a sequence.
All inputs are finite; a program needn't handle non-finite values.
Results may differ from the reference program's by a relative error of at most 0.017.
Values may be sent and summed in bfloat16 or wider, within the bound.
A program may use at most 192 MiB of HBM per device.

```python
import math
import jax
import jax.numpy as jnp
import numpy as np
from jax import lax

D = 768
HEADS = 12
HEAD_DIM = 64
FF = 3072
BUCKETS = 32
MAX_DISTANCE = 128
DOCS = 4
TOK_DEV = 512
EXPERTS = 8
CAP = 160
SEQS = 32
TOKENS = 16384
N_DP = 4
DEVICES = 32


def block_levels(own_key, dims, shards, smallest, largest):
    def one(position, parts):
        draws = jax.random.uniform(jax.random.fold_in(jax.random.fold_in(own_key, 6), position), (parts,), jnp.float32, smallest / len(shards), largest / len(shards))
        return jnp.repeat(jnp.exp(draws), dims[position] // parts).reshape((-1,) + (1,) * (len(dims) - position - 1))

    loudness = one(*shards[0])
    for cut in shards[1:]:
        loudness = loudness * one(*cut)
    return loudness


def split_up(count, total, bound, slope):
    portions = [(1 << 20) // math.isqrt(rank ** slope) + 1 for rank in range(2, count + 1)]
    rest, given = total - bound - (count - 1), [1] * (count - 1)
    while rest > 0:
        free = [i for i in range(count - 1) if given[i] < bound]
        mass, budget = sum([portions[i] for i in free]), rest
        for i in free:
            addition = min(bound - given[i], max(1, budget * portions[i] // mass), rest)
            given[i] = given[i] + addition
            rest = rest - addition
    return np.array([bound] + given)


def ragged(key, amount, total, reach, lean):
    if amount == 2:
        one = jax.random.randint(key, (), max(1, total - reach), min(reach, total - 1) + 1)
        return jnp.stack([one, total - one])
    sizes = jnp.asarray(split_up(amount, total, reach, lean), jnp.int32)
    pairs = (amount - 1) // 2
    source_of, sink = sizes[1:1 + 2 * pairs:2], sizes[2:2 + 2 * pairs:2]
    slack = jnp.minimum(source_of - 1, reach - sink)
    shifted = jax.random.randint(jax.random.fold_in(key, 1), (pairs,), 0, 1 << 20) % (slack + 1)
    sizes = sizes.at[1:1 + 2 * pairs:2].set(source_of - shifted).at[2:2 + 2 * pairs:2].set(sink + shifted)
    return sizes[jax.random.permutation(jax.random.fold_in(key, 2), amount)]


def deal_out(key, own, number, rows, amount, top, bound, slope):
    sequence = jax.random.permutation(key, amount)
    crowded, usual = load_shares(amount, rows * top, bound, slope, True), load_shares(amount, rows * top, bound, slope, False)
    places = jnp.arange(amount)

    def named(lengths, offset_by):
        used = int((lengths > 0).sum())
        fixed = max(1, used // 4)
        moved = fixed + (places - fixed + offset_by * (used - fixed)) % max(1, amount - fixed)
        return jnp.zeros((amount,), jnp.int32).at[sequence[jnp.where(places < fixed, places, moved)]].set(jnp.asarray(lengths, jnp.int32))

    lengths = jnp.where(number % 4 == 0, named(crowded, number // 4), named(usual, number - number // 4 - 1))
    mixed = jax.random.permutation(jax.random.fold_in(own, 3), amount)
    giver, receiver = mixed[0:amount // 2 * 2:2], mixed[1:amount // 2 * 2:2]
    slack = jnp.minimum(lengths[giver] - 1, bound - lengths[receiver]) // 2
    slack = jnp.where((giver == sequence[0]) | (receiver == sequence[0]) | (lengths[receiver] == 0), 0, jnp.maximum(slack, 0))
    moved = jax.random.randint(jax.random.fold_in(own, 4), (amount // 2,), 0, 1 << 20) % (slack + 1)
    lengths = lengths.at[giver].add(-moved).at[receiver].add(moved)
    labels = jnp.searchsorted(jnp.cumsum(lengths), jnp.arange(rows * top), side="right").astype(jnp.int32)
    grid = labels.reshape(top, rows).T
    grid = grid[jax.random.permutation(jax.random.fold_in(own, 1), rows)]
    offset_by = jax.random.randint(jax.random.fold_in(own, 2), (rows, 1), 0, top)
    return jnp.take_along_axis(grid, (jnp.arange(top)[None, :] + offset_by) % top, axis=1)


def load_shares(count, total, reach, skew, full):
    loads = [(1 << 20) // math.isqrt(standing ** skew) + 1 for standing in range(1, count + 1)]
    largest = reach if full else min(reach, max(-(-total // count), total * loads[0] // sum(loads)))
    least = 1 if total - largest >= count - 1 else 0
    given, spare = [largest] + [least] * (count - 1), total - largest - least * (count - 1)
    while spare > 0:
        candidates = [i for i in range(1, count) if given[i] < largest] or [i for i in range(1, count) if given[i] < reach]
        whole, budget = sum([loads[i] for i in candidates]), spare
        for i in candidates:
            more = min(reach - given[i], max(1, budget * loads[i] // whole), spare)
            given[i] = given[i] + more
            spare = spare - more
    return np.array(given)


def bell_draw(key, dims, width, reach, pieces=(), kind=jnp.bfloat16):
    gain = block_levels(key, dims, pieces, -0.22, 0.18) if pieces else 1.0
    array = jax.random.normal(key, dims, jnp.float32) * width * gain
    return jnp.minimum(jnp.maximum(array, -reach), reach).astype(kind)


def setup_inputs(seed: int = 0) -> dict:
    arg_keys = jax.random.split(jax.random.key(seed), 15)
    tokens = bell_draw(arg_keys[0], (TOKENS, D), 1.0, 6.0, ((0, 32),))
    cotangent = bell_draw(arg_keys[1], (TOKENS, D), 1.0, 6.0, ((0, 32),))
    segment_ids = jax.vmap(lambda own: jnp.searchsorted(jnp.cumsum(ragged(own, DOCS, TOK_DEV, TOK_DEV // 2, 0)), jnp.arange(TOK_DEV), side="right"))(jax.random.split(arg_keys[2], SEQS)).reshape((SEQS, TOK_DEV)).astype(jnp.int32)
    routes_keys = jax.random.split(jax.random.fold_in(arg_keys[3], 1), TOKENS // TOK_DEV)
    routes_turns = jax.random.permutation(jax.random.fold_in(arg_keys[3], 3), TOKENS // TOK_DEV)
    routes = jax.vmap(lambda own, number: deal_out(jax.random.fold_in(arg_keys[3], 2), own, number, TOK_DEV, EXPERTS, 2, CAP, 2))(routes_keys, routes_turns).reshape((TOKENS, 2))
    gain_attn = jnp.clip(1.0 + 0.18 * jax.random.normal(arg_keys[4], (D,), jnp.float32), 0.099609375, 1.8984375).astype(jnp.bfloat16)
    gain_ffn = jnp.clip(1.0 + 0.18 * jax.random.normal(arg_keys[5], (D,), jnp.float32), 0.099609375, 1.8984375).astype(jnp.bfloat16)
    w_query = bell_draw(arg_keys[6], (D, D), D ** -0.5, 0.21875, ((0, 2),))
    w_key = bell_draw(arg_keys[7], (D, D), D ** -0.5, 0.21875, ((0, 2),))
    w_value = bell_draw(arg_keys[8], (D, D), D ** -0.5, 0.21875, ((0, 2),))
    w_project = bell_draw(arg_keys[9], (D, D), (D // 16) ** -0.5, 0.875, ((0, 2),))
    router = bell_draw(arg_keys[10], (D, EXPERTS), (2 * D) ** -0.5, 0.15625, ((0, 2),))
    bias_table = bell_draw(arg_keys[11], (HEADS, BUCKETS), 1.0, 4.0, ((0, 2),))
    expert_in = bell_draw(arg_keys[12], (EXPERTS, D, FF), D ** -0.5, 0.21875, ((0, 8),))
    expert_out = bell_draw(arg_keys[13], (EXPERTS, FF, D), (FF // 4) ** -0.5, 0.21875, ((0, 8),))
    return {"tokens": tokens, "cotangent": cotangent, "segment_ids": segment_ids, "routes": routes, "gain_attn": gain_attn, "gain_ffn": gain_ffn, "w_query": w_query, "w_key": w_key, "w_value": w_value, "w_project": w_project, "router": router, "bias_table": bias_table, "expert_in": expert_in, "expert_out": expert_out}


EPS = 1e-06
HIGH = lax.Precision.HIGHEST

@jax.custom_vjp
def low(v):
    return lax.optimization_barrier(v.astype(jnp.bfloat16)).astype(jnp.float32)

@jax.custom_vjp
def low_back(v):
    return v

def low_keep(v):
    return (low(v), None)

def low_pass(kept, grad):
    return (grad,)

def back_keep(v):
    return (v, None)

def back_low(kept, grad):
    return (low(grad),)
low.defvjp(low_keep, low_pass)
low_back.defvjp(back_keep, back_low)

def bucket_edges():
    half = BUCKETS // 2
    spans = np.arange(half, MAX_DISTANCE)
    levels = half + np.floor(np.log(spans / float(half)) / np.log(MAX_DISTANCE / float(half)) * half).astype(np.int64)
    return [int(spans[levels >= level][0]) for level in range(half + 1, BUCKETS) if np.any(levels >= level)]

def bucket_of(distance):
    distance = jnp.maximum(distance, 0)
    bucket = jnp.minimum(distance, BUCKETS // 2)
    for edge in bucket_edges():
        bucket = bucket + (distance >= edge).astype(jnp.int32)
    return bucket

def attend(queries, key_rows, value_rows, segment, table):
    length = queries.shape[0]
    places = jnp.arange(length, dtype=jnp.int32)
    distance = places[:, None] - places[None, :]
    allowed = (distance >= 0) & (segment[:, None] == segment[None, :])
    bias = table[:, bucket_of(distance)]
    scores = jnp.einsum('qhd,khd->hqk', queries, key_rows, precision=HIGH) * HEAD_DIM ** (-0.5) + bias
    scores = low_back(scores)
    masked = jnp.where(allowed[None], scores, -1e+30)
    highest = lax.optimization_barrier(jnp.max(masked, axis=-1, keepdims=True))
    expo = jnp.exp(masked - highest)
    probs = expo / lax.optimization_barrier(jnp.sum(expo, axis=-1, keepdims=True))
    return jnp.einsum('hqk,khd->qhd', low(probs), value_rows, precision=HIGH)

def expert_apply(inputs):
    rows, weight_in, weight_out = inputs
    pre = low_back(jnp.dot(rows, weight_in, precision=HIGH))
    hidden = low(jax.nn.gelu(pre))
    return low_back(low(jnp.dot(hidden, weight_out, precision=HIGH)))

def layer(tokens, gain_attn, gain_ffn, w_query, w_key, w_value, w_project, router, table, expert_in, expert_out, segment_ids, routes, dest):
    rms_one = lax.rsqrt(lax.optimization_barrier(jnp.mean(tokens * tokens, axis=-1, keepdims=True)) + EPS)
    normed = low(tokens * rms_one * gain_attn)

    def project(weight):
        return low_back(low(jnp.dot(normed, weight, precision=HIGH))).reshape(SEQS, TOK_DEV, HEADS, HEAD_DIM)
    queries, key_rows, value_rows = (project(w_query), project(w_key), project(w_value))
    checked = jax.checkpoint(attend)
    attended = lax.map(lambda inputs: checked(inputs[0], inputs[1], inputs[2], inputs[3], table), (queries, key_rows, value_rows, segment_ids))
    attended = low_back(low(attended.reshape(TOKENS, D)))
    branch = low_back(jnp.dot(attended, w_project, precision=HIGH))
    resid = tokens + branch
    rms_two = lax.rsqrt(lax.optimization_barrier(jnp.mean(resid * resid, axis=-1, keepdims=True)) + EPS)
    normed_two = low(resid * rms_two * gain_ffn)
    logits = low_back(jnp.dot(normed_two, router, precision=HIGH))
    chosen = jnp.take_along_axis(logits, routes, axis=1)
    gates = jax.nn.softmax(chosen, axis=-1)
    copies = jnp.repeat(normed_two, 2, axis=0)
    buffer = jnp.zeros((N_DP * EXPERTS * EXPERTS * CAP, D), jnp.float32).at[dest].set(copies)
    buffer = low_back(buffer)
    per_expert = buffer.reshape(N_DP, EXPERTS, EXPERTS * CAP, D).transpose(1, 0, 2, 3).reshape(EXPERTS, N_DP * EXPERTS * CAP, D)
    results = lax.map(jax.checkpoint(expert_apply), (per_expert, expert_in, expert_out))
    returned = results.reshape(EXPERTS, N_DP, EXPERTS * CAP, D).transpose(1, 0, 2, 3).reshape(-1, D)
    picked = returned[dest].reshape(TOKENS, 2, D)
    return resid + lax.optimization_barrier(jnp.sum(gates[..., None] * picked, axis=1))

def reference(tokens, cotangent, segment_ids, routes, gain_attn, gain_ffn, w_query, w_key, w_value, w_project, router, bias_table, expert_in, expert_out):
    flat = routes.reshape(-1).astype(jnp.int32)
    onehot = (flat[:, None] == jnp.arange(EXPERTS, dtype=jnp.int32)[None, :]).astype(jnp.int32)
    onehot = onehot.reshape(DEVICES, 2 * TOK_DEV, EXPERTS)
    slot_place = (lax.optimization_barrier(jnp.sum(jnp.cumsum(onehot, axis=1) * onehot, axis=-1)).reshape(-1) - 1).astype(jnp.int32)
    device = (jnp.arange(2 * TOKENS, dtype=jnp.int32) // (2 * TOK_DEV)).astype(jnp.int32)
    dest = (((device // EXPERTS * EXPERTS + flat) * EXPERTS + device % EXPERTS) * CAP + slot_place).astype(jnp.int32)
    floats = [a.astype(jnp.float32) for a in (tokens, gain_attn, gain_ffn, w_query, w_key, w_value, w_project, router, bias_table, expert_in, expert_out)]

    def forward(*values):
        return layer(*values, segment_ids, routes, dest)
    output, pullback = jax.vjp(forward, *floats)
    grads = pullback(cotangent.astype(jnp.float32))
    return (output.astype(jnp.bfloat16), grads[0], grads[1], grads[2], grads[3], grads[4], grads[5], grads[6], grads[7], grads[8], grads[9], grads[10])
```

```python
import jax
import jax.numpy as jnp
import numpy as np
from jax import lax
from jax.sharding import PartitionSpec as P

BUCKETS = 32
MAX_DISTANCE = 128


EPS = 1e-06


def bucket_edges():
    half = BUCKETS // 2
    spans = np.arange(half, MAX_DISTANCE)
    levels = half + np.floor(
        np.log(spans / float(half)) / np.log(MAX_DISTANCE / float(half)) * half
    ).astype(np.int64)
    return [
        int(spans[levels >= level][0])
        for level in range(half + 1, BUCKETS)
        if np.any(levels >= level)
    ]


def bucket_of(distance):
    distance = jnp.maximum(distance, 0)
    bucket = jnp.minimum(distance, BUCKETS // 2)
    for edge in bucket_edges():
        bucket = bucket + (distance >= edge).astype(jnp.int32)
    return bucket


def contract(left, right, left_dim, right_dim):
    return lax.dot_general(
        left, right, (((left_dim,), (right_dim,)), ((), ())), preferred_element_type=jnp.float32
    )


def send_rows(rows):
    moved = lax.all_to_all(rows, ("expert", "wshard"), split_axis=0, concat_axis=0, tiled=True)
    return moved


def send_results(rows):
    moved = lax.all_to_all(rows, ("expert", "wshard"), split_axis=0, concat_axis=0, tiled=True)
    return moved


def send_grads(rows):
    moved = lax.all_to_all(rows, ("expert", "wshard"), split_axis=0, concat_axis=0, tiled=True)
    return moved


def send_row_grads(rows):
    moved = lax.all_to_all(rows, ("expert", "wshard"), split_axis=0, concat_axis=0, tiled=True)
    return moved


def block_scores(query_block, key_rows, start, segment, table, block, length, scale):
    rows = start + jnp.arange(block, dtype=jnp.int32)
    distance = rows[:, None] - jnp.arange(length, dtype=jnp.int32)[None, :]
    allowed = (distance >= 0) & (segment[:, None] == segment[None, :])
    onehot = (bucket_of(distance)[..., None] == jnp.arange(BUCKETS, dtype=jnp.int32)).astype(
        jnp.bfloat16
    )
    bias = jnp.einsum("qkb,hb->hqk", onehot, table, preferred_element_type=jnp.float32)
    raw = jnp.einsum("qhd,khd->hqk", query_block, key_rows, preferred_element_type=jnp.float32)
    scores = raw * scale + bias
    return (jnp.where(allowed[None], scores, -1e30), onehot)


def norm_back(grad_normed, inputs, rms, gain):
    unit = inputs * rms
    grad_gain = jnp.sum(grad_normed * unit, axis=0)
    scaled = grad_normed * gain
    return (grad_gain, rms * (scaled - unit * jnp.mean(scaled * unit, axis=-1, keepdims=True)))


def per_device(
    tokens,
    cotangent,
    segment_ids,
    routes,
    gain_attn,
    gain_ffn,
    w_query,
    w_key,
    w_value,
    w_project,
    router,
    bias_table,
    expert_in,
    expert_out,
):
    gathered = (
        lax.all_gather(gain_attn, "wshard", axis=0, tiled=True),
        lax.all_gather(gain_ffn, "wshard", axis=0, tiled=True),
        lax.all_gather(w_query, "wshard", axis=0, tiled=True),
        lax.all_gather(w_key, "wshard", axis=0, tiled=True),
        lax.all_gather(w_value, "wshard", axis=0, tiled=True),
        lax.all_gather(w_project, "wshard", axis=0, tiled=True),
        lax.all_gather(router, "wshard", axis=0, tiled=True),
        lax.all_gather(bias_table, "wshard", axis=0, tiled=True),
    )
    gain_one, gain_two, query_full, key_full, value_full, project_full, router_full, table_full = (
        gathered
    )
    gain_one = gain_one.astype(jnp.float32)
    gain_two = gain_two.astype(jnp.float32)
    length, width = tokens.shape
    heads = table_full.shape[0]
    head_size = width // heads
    experts = router_full.shape[1]
    capacity = 5 * length // (2 * experts)
    block = min(512, length)
    scale = head_size ** (-0.5)
    segment = segment_ids[0]
    starts = jnp.arange(length // block, dtype=jnp.int32) * block
    flat = routes.reshape(-1)
    onehot_int = (flat[:, None] == jnp.arange(experts, dtype=jnp.int32)[None, :]).astype(jnp.int32)
    slot_place = jnp.sum(jnp.cumsum(onehot_int, axis=0) * onehot_int, axis=-1) - 1
    dest = (flat * capacity + slot_place).reshape(length, 2)
    slots = jnp.arange(experts * capacity, dtype=jnp.int32)
    takes_first = slots[:, None] == dest[None, :, 0]
    takes_second = slots[:, None] == dest[None, :, 1]
    spread = (takes_first | takes_second).astype(jnp.bfloat16)
    pick_first = (dest[:, 0][:, None] == slots[None, :]).astype(jnp.bfloat16)
    pick_second = (dest[:, 1][:, None] == slots[None, :]).astype(jnp.bfloat16)

    def to_slots(rows):
        placed = jnp.dot(spread, rows, preferred_element_type=jnp.float32).astype(jnp.bfloat16)
        return placed.reshape(experts, capacity, width)

    cotangent_arrived = send_grads(to_slots(cotangent)).reshape(-1, width)
    inputs = tokens.astype(jnp.float32)
    rms_one = lax.rsqrt(jnp.mean(inputs * inputs, axis=-1, keepdims=True) + EPS)
    normed = (inputs * rms_one * gain_one).astype(jnp.bfloat16)
    joined_weight = jnp.concatenate([query_full, key_full, value_full], axis=1)
    projected = jnp.dot(normed, joined_weight, preferred_element_type=jnp.float32).astype(
        jnp.bfloat16
    )
    queries = projected[:, :width].reshape(length, heads, head_size)
    key_rows = projected[:, width : 2 * width].reshape(length, heads, head_size)
    value_rows = projected[:, 2 * width :].reshape(length, heads, head_size)

    def forward_block(start):
        masked, onehot = block_scores(
            queries, key_rows, start, segment, table_full, block, length, scale
        )
        highest = jnp.max(masked, axis=-1, keepdims=True)
        expo = jnp.exp(masked - highest)
        total = jnp.sum(expo, axis=-1, keepdims=True)
        probs = expo / total
        logsum = highest[..., 0] + jnp.log(total[..., 0])
        result = jnp.einsum(
            "hqk,khd->qhd",
            probs.astype(jnp.bfloat16),
            value_rows,
            preferred_element_type=jnp.float32,
        )
        return (result, logsum)

    attended, logsums = lax.map(forward_block, starts)
    attended = attended.reshape(length, width).astype(jnp.bfloat16)
    branch = jnp.dot(attended, project_full, preferred_element_type=jnp.float32)
    resid = inputs + branch
    rms_two = lax.rsqrt(jnp.mean(resid * resid, axis=-1, keepdims=True) + EPS)
    normed_two = (resid * rms_two * gain_two).astype(jnp.bfloat16)
    logits = jnp.dot(normed_two, router_full, preferred_element_type=jnp.float32)
    chosen_mask = routes[..., None] == jnp.arange(experts, dtype=jnp.int32)
    chosen = jnp.sum(jnp.where(chosen_mask, logits[:, None, :], 0.0), axis=-1)
    gates = jax.nn.softmax(chosen, axis=-1)
    normed_two, cotangent_arrived = lax.optimization_barrier((normed_two, cotangent_arrived))
    arrived = send_rows(to_slots(normed_two))
    gate_slots = jnp.sum(
        jnp.where(takes_first, gates[:, 0][None, :], 0.0)
        + jnp.where(takes_second, gates[:, 1][None, :], 0.0),
        axis=1,
    )
    gate_arrived = send_rows(gate_slots.reshape(experts, capacity)).reshape(-1)
    arrived, gate_arrived = lax.optimization_barrier((arrived, gate_arrived))
    rows_in = arrived.reshape(-1, width)
    pre = jnp.dot(rows_in, expert_in[0], preferred_element_type=jnp.float32)
    hidden = jax.nn.gelu(pre).astype(jnp.bfloat16)
    produced = jnp.dot(hidden, expert_out[0], preferred_element_type=jnp.float32).astype(
        jnp.bfloat16
    )
    returned = send_results(produced.reshape(experts, capacity, width)).reshape(-1, width)
    grad_arrived = (gate_arrived[:, None] * cotangent_arrived.astype(jnp.float32)).astype(
        jnp.bfloat16
    )
    grad_out_weight = contract(hidden, grad_arrived, 0, 0).astype(jnp.bfloat16)
    grad_hidden = contract(grad_arrived, expert_out[0], 1, 1)
    unused, gelu_back = jax.vjp(jax.nn.gelu, pre)
    grad_pre = gelu_back(grad_hidden)[0].astype(jnp.bfloat16)
    grad_in_weight = contract(rows_in, grad_pre, 0, 0).astype(jnp.bfloat16)
    grad_pre, grad_in_weight, grad_out_weight = lax.optimization_barrier(
        (grad_pre, grad_in_weight, grad_out_weight)
    )
    expert_out_sum = lax.psum_scatter(
        grad_out_weight[None], "dp", scatter_dimension=1, tiled=True
    )
    expert_in_sum = lax.psum_scatter(grad_in_weight[None], "dp", scatter_dimension=2, tiled=True)
    grad_rows = contract(grad_pre, expert_in[0], 1, 1).astype(jnp.bfloat16)
    returned, grad_rows = lax.optimization_barrier((returned, grad_rows))
    grad_back = send_row_grads(grad_rows.reshape(experts, capacity, width)).reshape(-1, width)
    picked_first = jnp.dot(pick_first, returned, preferred_element_type=jnp.float32)
    picked_second = jnp.dot(pick_second, returned, preferred_element_type=jnp.float32)
    mixed = resid + (gates[:, :1] * picked_first + gates[:, 1:] * picked_second)
    grad_out = cotangent.astype(jnp.float32)
    grad_gates = jnp.stack(
        [jnp.sum(grad_out * picked_first, axis=-1), jnp.sum(grad_out * picked_second, axis=-1)],
        axis=-1,
    )
    grad_normed_two = jnp.dot(
        pick_first + pick_second, grad_back, preferred_element_type=jnp.float32
    )
    grad_chosen = gates * (grad_gates - jnp.sum(gates * grad_gates, axis=-1, keepdims=True))
    grad_logits = jnp.sum(jnp.where(chosen_mask, grad_chosen[..., None], 0.0), axis=1).astype(
        jnp.bfloat16
    )
    grad_router = contract(normed_two, grad_logits, 0, 0)
    grad_normed_two = grad_normed_two + contract(grad_logits, router_full, 1, 1)
    grad_gain_two, grad_resid_norm = norm_back(grad_normed_two, resid, rms_two, gain_two)
    grad_resid = grad_out + grad_resid_norm
    grad_branch = grad_resid.astype(jnp.bfloat16)
    grad_project = contract(attended, grad_branch, 0, 0)
    grad_attended = (
        contract(grad_branch, project_full, 1, 1)
        .astype(jnp.bfloat16)
        .reshape(length, heads, head_size)
    )

    def backward_block(carry, inputs_block):
        grad_keys, grad_values, grad_table = carry
        start, logsum = inputs_block
        masked, onehot = block_scores(
            queries, key_rows, start, segment, table_full, block, length, scale
        )
        probs = jnp.exp(masked - logsum[..., None])
        grad_probs = jnp.einsum(
            "qhd,khd->hqk", grad_attended, value_rows, preferred_element_type=jnp.float32
        )
        inner = jnp.sum(probs * grad_probs, axis=-1, keepdims=True)
        grad_scores = (probs * (grad_probs - inner)).astype(jnp.bfloat16)
        grad_query_block = (
            jnp.einsum("hqk,khd->qhd", grad_scores, key_rows, preferred_element_type=jnp.float32)
            * scale
        )
        grad_keys = (
            grad_keys
            + jnp.einsum("hqk,qhd->khd", grad_scores, queries, preferred_element_type=jnp.float32)
            * scale
        )
        grad_values = grad_values + jnp.einsum(
            "hqk,qhd->khd",
            probs.astype(jnp.bfloat16),
            grad_attended,
            preferred_element_type=jnp.float32,
        )
        grad_table = grad_table + jnp.einsum(
            "hqk,qkb->hb", grad_scores, onehot, preferred_element_type=jnp.float32
        )
        return ((grad_keys, grad_values, grad_table), grad_query_block)

    zero_rows = jnp.zeros((length, heads, head_size), jnp.float32)
    start_carry = (zero_rows, zero_rows, jnp.zeros((heads, BUCKETS), jnp.float32))
    (grad_keys, grad_values, grad_table), grad_queries = lax.scan(
        backward_block, start_carry, (starts, logsums)
    )
    grad_joined = jnp.concatenate(
        [
            grad_queries.reshape(length, width),
            grad_keys.reshape(length, width),
            grad_values.reshape(length, width),
        ],
        axis=1,
    ).astype(jnp.bfloat16)
    grad_weights = contract(normed, grad_joined, 0, 0)
    grad_normed = contract(grad_joined, joined_weight, 1, 1)
    grad_gain_one, grad_input_norm = norm_back(grad_normed, inputs, rms_one, gain_one)
    grad_tokens = grad_resid + grad_input_norm
    half = width // 2
    small = jnp.concatenate(
        [grad_gain_one, grad_gain_two, grad_router.reshape(-1), grad_table.reshape(-1)]
    )
    large = jnp.stack(
        [
            grad_weights[:, :width],
            grad_weights[:, width : 2 * width],
            grad_weights[:, 2 * width :],
            grad_project,
        ]
    ).astype(jnp.bfloat16)
    large = large.reshape(4, 2, half, width).transpose(1, 0, 2, 3).reshape(2, 4 * half, width)
    core = lax.axis_index("wshard")
    keep = lax.dynamic_index_in_dim(large, core, 0, keepdims=False)
    give = lax.dynamic_index_in_dim(large, 1 - core, 0, keepdims=False)
    got = lax.ppermute(give, "wshard", [(0, 1), (1, 0)])
    part = (keep.astype(jnp.float32) + got.astype(jnp.float32)).astype(jnp.bfloat16)
    for axis in ("dp", "expert"):
        pieces = lax.all_to_all(
            part.reshape(lax.axis_size(axis), -1, width), axis, split_axis=0, concat_axis=0, tiled=True
        )
        part = jnp.sum(pieces.astype(jnp.float32), axis=0).astype(jnp.bfloat16)
    for axis in ("expert", "dp"):
        part = lax.all_gather(part, axis, axis=0, tiled=True)
    part = part.reshape(4, half, width).astype(jnp.float32)
    small = lax.psum(small, ("dp", "expert", "wshard"))
    edges = np.cumsum([0, width, width, width * experts, heads * BUCKETS])

    def own(index, shape):
        piece = small[edges[index] : edges[index + 1]].reshape(shape)
        rows = shape[0] // 2
        return lax.dynamic_slice_in_dim(piece, core * rows, rows, 0)

    shares = (
        own(0, (width,)),
        own(1, (width,)),
        part[0],
        part[1],
        part[2],
        part[3],
        own(2, (width, experts)),
        own(3, (heads, BUCKETS)),
    )
    expert_in_grad = expert_in_sum.astype(jnp.float32)
    expert_out_grad = expert_out_sum.astype(jnp.float32)
    return (
        mixed.astype(jnp.bfloat16),
        grad_tokens,
        shares[0],
        shares[1],
        shares[2],
        shares[3],
        shares[4],
        shares[5],
        shares[6],
        shares[7],
        expert_in_grad,
        expert_out_grad,
    )


def solution(mesh):
    return jax.shard_map(
        per_device,
        mesh=mesh,
        in_specs=(
            P(("dp", "expert", "wshard"), None),
            P(("dp", "expert", "wshard"), None),
            P(("dp", "expert", "wshard"), None),
            P(("dp", "expert", "wshard"), None),
            P("wshard"),
            P("wshard"),
            P("wshard", None),
            P("wshard", None),
            P("wshard", None),
            P("wshard", None),
            P("wshard", None),
            P("wshard", None),
            P(("expert", "wshard"), None, None),
            P(("expert", "wshard"), None, None),
        ),
        out_specs=(
            P(("dp", "expert", "wshard"), None),
            P(("dp", "expert", "wshard"), None),
            P("wshard"),
            P("wshard"),
            P("wshard", None),
            P("wshard", None),
            P("wshard", None),
            P("wshard", None),
            P("wshard", None),
            P("wshard", None),
            P(("expert", "wshard"), None, "dp"),
            P(("expert", "wshard"), "dp", None),
        ),
        check_vma=False,
    )
```

```python
import jax
import jax.numpy as jnp
import numpy as np
from jax import lax
from jax.sharding import PartitionSpec as P

BUCKETS = 32
MAX_DISTANCE = 128


EPS = 1e-06


def bucket_edges():
    half = BUCKETS // 2
    spans = np.arange(half, MAX_DISTANCE)
    levels = half + np.floor(
        np.log(spans / float(half)) / np.log(MAX_DISTANCE / float(half)) * half
    ).astype(np.int64)
    return [
        int(spans[levels >= level][0])
        for level in range(half + 1, BUCKETS)
        if np.any(levels >= level)
    ]


def bucket_of(distance):
    distance = jnp.maximum(distance, 0)
    bucket = jnp.minimum(distance, BUCKETS // 2)
    for edge in bucket_edges():
        bucket = bucket + (distance >= edge).astype(jnp.int32)
    return bucket


def contract(left, right, left_dim, right_dim):
    return lax.dot_general(
        left, right, (((left_dim,), (right_dim,)), ((), ())), preferred_element_type=jnp.float32
    )


def send_rows(rows):
    moved = lax.all_to_all(rows, ("expert", "wshard"), split_axis=0, concat_axis=0, tiled=True)
    return moved


def send_results(rows):
    moved = lax.all_to_all(rows, ("expert", "wshard"), split_axis=0, concat_axis=0, tiled=True)
    return moved


def send_grads(rows):
    moved = lax.all_to_all(rows, ("expert", "wshard"), split_axis=0, concat_axis=0, tiled=True)
    return moved


def send_row_grads(rows):
    moved = lax.all_to_all(rows, ("expert", "wshard"), split_axis=0, concat_axis=0, tiled=True)
    return moved


def block_scores(query_block, key_rows, start, segment, table, block, length, scale):
    rows = start + jnp.arange(block, dtype=jnp.int32)
    distance = rows[:, None] - jnp.arange(length, dtype=jnp.int32)[None, :]
    allowed = (distance >= 0) & (segment[:, None] == segment[None, :])
    onehot = (bucket_of(distance)[..., None] == jnp.arange(BUCKETS, dtype=jnp.int32)).astype(
        jnp.bfloat16
    )
    bias = jnp.einsum("qkb,hb->hqk", onehot, table, preferred_element_type=jnp.float32)
    raw = jnp.einsum("qhd,khd->hqk", query_block, key_rows, preferred_element_type=jnp.float32)
    scores = raw * scale + bias
    return (jnp.where(allowed[None], scores, -1e30), onehot)


def norm_back(grad_normed, inputs, rms, gain):
    unit = inputs * rms
    grad_gain = jnp.sum(grad_normed * unit, axis=0)
    scaled = grad_normed * gain
    return (grad_gain, rms * (scaled - unit * jnp.mean(scaled * unit, axis=-1, keepdims=True)))


def per_device(
    tokens,
    cotangent,
    segment_ids,
    routes,
    gain_attn,
    gain_ffn,
    w_query,
    w_key,
    w_value,
    w_project,
    router,
    bias_table,
    expert_in,
    expert_out,
):
    gathered = (
        lax.all_gather(gain_attn, "wshard", axis=0, tiled=True),
        lax.all_gather(gain_ffn, "wshard", axis=0, tiled=True),
        lax.all_gather(w_query, "wshard", axis=0, tiled=True),
        lax.all_gather(w_key, "wshard", axis=0, tiled=True),
        lax.all_gather(w_value, "wshard", axis=0, tiled=True),
        lax.all_gather(w_project, "wshard", axis=0, tiled=True),
        lax.all_gather(router, "wshard", axis=0, tiled=True),
        lax.all_gather(bias_table, "wshard", axis=0, tiled=True),
    )
    gain_one, gain_two, query_full, key_full, value_full, project_full, router_full, table_full = (
        gathered
    )
    gain_one = gain_one.astype(jnp.float32)
    gain_two = gain_two.astype(jnp.float32)
    length, width = tokens.shape
    heads = table_full.shape[0]
    head_size = width // heads
    experts = router_full.shape[1]
    capacity = 5 * length // (2 * experts)
    block = min(512, length)
    scale = head_size ** (-0.5)
    segment = segment_ids[0]
    starts = jnp.arange(length // block, dtype=jnp.int32) * block
    flat = routes.reshape(-1)
    onehot_int = (flat[:, None] == jnp.arange(experts, dtype=jnp.int32)[None, :]).astype(jnp.int32)
    slot_place = jnp.sum(jnp.cumsum(onehot_int, axis=0) * onehot_int, axis=-1) - 1
    dest = (flat * capacity + slot_place).reshape(length, 2)
    slots = jnp.arange(experts * capacity, dtype=jnp.int32)
    takes_first = slots[:, None] == dest[None, :, 0]
    takes_second = slots[:, None] == dest[None, :, 1]
    spread = (takes_first | takes_second).astype(jnp.bfloat16)
    pick_first = (dest[:, 0][:, None] == slots[None, :]).astype(jnp.bfloat16)
    pick_second = (dest[:, 1][:, None] == slots[None, :]).astype(jnp.bfloat16)

    def to_slots(rows):
        placed = jnp.dot(spread, rows, preferred_element_type=jnp.float32).astype(jnp.bfloat16)
        return placed.reshape(experts, capacity, width)

    cotangent_arrived = send_grads(to_slots(cotangent)).reshape(-1, width)
    inputs = tokens.astype(jnp.float32)
    rms_one = lax.rsqrt(jnp.mean(inputs * inputs, axis=-1, keepdims=True) + EPS)
    normed = (inputs * rms_one * gain_one).astype(jnp.bfloat16)
    joined_weight = jnp.concatenate([query_full, key_full, value_full], axis=1)
    projected = jnp.dot(normed, joined_weight, preferred_element_type=jnp.float32).astype(
        jnp.bfloat16
    )
    queries = projected[:, :width].reshape(length, heads, head_size)
    key_rows = projected[:, width : 2 * width].reshape(length, heads, head_size)
    value_rows = projected[:, 2 * width :].reshape(length, heads, head_size)

    def forward_block(start):
        masked, onehot = block_scores(
            queries, key_rows, start, segment, table_full, block, length, scale
        )
        highest = jnp.max(masked, axis=-1, keepdims=True)
        expo = jnp.exp(masked - highest)
        total = jnp.sum(expo, axis=-1, keepdims=True)
        probs = expo / total
        logsum = highest[..., 0] + jnp.log(total[..., 0])
        result = jnp.einsum(
            "hqk,khd->qhd",
            probs.astype(jnp.bfloat16),
            value_rows,
            preferred_element_type=jnp.float32,
        )
        return (result, logsum)

    attended, logsums = lax.map(forward_block, starts)
    attended = attended.reshape(length, width).astype(jnp.bfloat16)
    branch = jnp.dot(attended, project_full, preferred_element_type=jnp.float32)
    resid = inputs + branch
    rms_two = lax.rsqrt(jnp.mean(resid * resid, axis=-1, keepdims=True) + EPS)
    normed_two = (resid * rms_two * gain_two).astype(jnp.bfloat16)
    logits = jnp.dot(normed_two, router_full, preferred_element_type=jnp.float32)
    chosen_mask = routes[..., None] == jnp.arange(experts, dtype=jnp.int32)
    chosen = jnp.sum(jnp.where(chosen_mask, logits[:, None, :], 0.0), axis=-1)
    gates = jax.nn.softmax(chosen, axis=-1)
    normed_two, cotangent_arrived = lax.optimization_barrier((normed_two, cotangent_arrived))
    arrived = send_rows(to_slots(normed_two))
    gate_slots = jnp.sum(
        jnp.where(takes_first, gates[:, 0][None, :], 0.0)
        + jnp.where(takes_second, gates[:, 1][None, :], 0.0),
        axis=1,
    )
    gate_arrived = send_rows(gate_slots.reshape(experts, capacity)).reshape(-1)
    arrived, gate_arrived = lax.optimization_barrier((arrived, gate_arrived))
    rows_in = arrived.reshape(-1, width)
    pre = jnp.dot(rows_in, expert_in[0], preferred_element_type=jnp.float32)
    hidden = jax.nn.gelu(pre).astype(jnp.bfloat16)
    produced = jnp.dot(hidden, expert_out[0], preferred_element_type=jnp.float32).astype(
        jnp.bfloat16
    )
    produced, gate_arrived = lax.optimization_barrier((produced, gate_arrived))
    returned = send_results(produced.reshape(experts, capacity, width)).reshape(-1, width)
    grad_arrived = (gate_arrived[:, None] * cotangent_arrived.astype(jnp.float32)).astype(
        jnp.bfloat16
    )
    grad_out_weight = contract(hidden, grad_arrived, 0, 0).astype(jnp.bfloat16)
    grad_hidden = contract(grad_arrived, expert_out[0], 1, 1)
    unused, gelu_back = jax.vjp(jax.nn.gelu, pre)
    grad_pre = gelu_back(grad_hidden)[0].astype(jnp.bfloat16)
    grad_in_weight = contract(rows_in, grad_pre, 0, 0).astype(jnp.bfloat16)
    grad_pre, grad_in_weight, grad_out_weight = lax.optimization_barrier(
        (grad_pre, grad_in_weight, grad_out_weight)
    )
    expert_out_sum = lax.psum_scatter(
        grad_out_weight[None], "dp", scatter_dimension=1, tiled=True
    )
    expert_in_sum = lax.psum_scatter(grad_in_weight[None], "dp", scatter_dimension=2, tiled=True)
    grad_rows = contract(grad_pre, expert_in[0], 1, 1).astype(jnp.bfloat16)
    returned, grad_rows = lax.optimization_barrier((returned, grad_rows))
    grad_back = send_row_grads(grad_rows.reshape(experts, capacity, width)).reshape(-1, width)
    picked_first = jnp.dot(pick_first, returned, preferred_element_type=jnp.float32)
    picked_second = jnp.dot(pick_second, returned, preferred_element_type=jnp.float32)
    mixed = resid + (gates[:, :1] * picked_first + gates[:, 1:] * picked_second)
    grad_out = cotangent.astype(jnp.float32)
    grad_gates = jnp.stack(
        [jnp.sum(grad_out * picked_first, axis=-1), jnp.sum(grad_out * picked_second, axis=-1)],
        axis=-1,
    )
    grad_normed_two = jnp.dot(
        pick_first + pick_second, grad_back, preferred_element_type=jnp.float32
    )
    grad_chosen = gates * (grad_gates - jnp.sum(gates * grad_gates, axis=-1, keepdims=True))
    grad_logits = jnp.sum(jnp.where(chosen_mask, grad_chosen[..., None], 0.0), axis=1).astype(
        jnp.bfloat16
    )
    grad_router = contract(normed_two, grad_logits, 0, 0)
    grad_normed_two = grad_normed_two + contract(grad_logits, router_full, 1, 1)
    grad_gain_two, grad_resid_norm = norm_back(grad_normed_two, resid, rms_two, gain_two)
    grad_resid = grad_out + grad_resid_norm
    grad_branch = grad_resid.astype(jnp.bfloat16)
    grad_project = contract(attended, grad_branch, 0, 0)
    grad_attended = (
        contract(grad_branch, project_full, 1, 1)
        .astype(jnp.bfloat16)
        .reshape(length, heads, head_size)
    )

    def backward_block(carry, inputs_block):
        grad_keys, grad_values, grad_table = carry
        start, logsum = inputs_block
        masked, onehot = block_scores(
            queries, key_rows, start, segment, table_full, block, length, scale
        )
        probs = jnp.exp(masked - logsum[..., None])
        grad_probs = jnp.einsum(
            "qhd,khd->hqk", grad_attended, value_rows, preferred_element_type=jnp.float32
        )
        inner = jnp.sum(probs * grad_probs, axis=-1, keepdims=True)
        grad_scores = (probs * (grad_probs - inner)).astype(jnp.bfloat16)
        grad_query_block = (
            jnp.einsum("hqk,khd->qhd", grad_scores, key_rows, preferred_element_type=jnp.float32)
            * scale
        )
        grad_keys = (
            grad_keys
            + jnp.einsum("hqk,qhd->khd", grad_scores, queries, preferred_element_type=jnp.float32)
            * scale
        )
        grad_values = grad_values + jnp.einsum(
            "hqk,qhd->khd",
            probs.astype(jnp.bfloat16),
            grad_attended,
            preferred_element_type=jnp.float32,
        )
        grad_table = grad_table + jnp.einsum(
            "hqk,qkb->hb", grad_scores, onehot, preferred_element_type=jnp.float32
        )
        return ((grad_keys, grad_values, grad_table), grad_query_block)

    zero_rows = jnp.zeros((length, heads, head_size), jnp.float32)
    start_carry = (zero_rows, zero_rows, jnp.zeros((heads, BUCKETS), jnp.float32))
    (grad_keys, grad_values, grad_table), grad_queries = lax.scan(
        backward_block, start_carry, (starts, logsums)
    )
    grad_joined = jnp.concatenate(
        [
            grad_queries.reshape(length, width),
            grad_keys.reshape(length, width),
            grad_values.reshape(length, width),
        ],
        axis=1,
    ).astype(jnp.bfloat16)
    grad_weights = contract(normed, grad_joined, 0, 0)
    grad_normed = contract(grad_joined, joined_weight, 1, 1)
    grad_gain_one, grad_input_norm = norm_back(grad_normed, inputs, rms_one, gain_one)
    grad_tokens = grad_resid + grad_input_norm
    half = width // 2
    group = lax.axis_size("dp") * lax.axis_size("expert") * 8
    small = jnp.concatenate(
        [
            grad_gain_one.reshape(2, -1),
            grad_gain_two.reshape(2, -1),
            grad_router.reshape(2, -1),
            grad_table.reshape(2, -1),
        ],
        axis=1,
    ).astype(jnp.bfloat16)
    edges = np.cumsum([0, half, half, half * experts, heads // 2 * BUCKETS])
    extra = -(-int(edges[-1]) // (group * width)) * group
    small = jnp.pad(small, ((0, 0), (0, extra * width - int(edges[-1])))).reshape(2, extra, width)
    large = jnp.stack(
        [
            grad_weights[:, :width],
            grad_weights[:, width : 2 * width],
            grad_weights[:, 2 * width :],
            grad_project,
        ]
    ).astype(jnp.bfloat16)
    large = large.reshape(4, 2, half, width).transpose(1, 0, 2, 3).reshape(2, 4 * half, width)
    large = jnp.concatenate([large, small], axis=1)
    core = lax.axis_index("wshard")
    keep = lax.dynamic_index_in_dim(large, core, 0, keepdims=False)
    give = lax.dynamic_index_in_dim(large, 1 - core, 0, keepdims=False)
    got = lax.ppermute(give, "wshard", [(0, 1), (1, 0)])
    part = (keep.astype(jnp.float32) + got.astype(jnp.float32)).astype(jnp.bfloat16)
    for axis in ("dp", "expert"):
        pieces = lax.all_to_all(
            part.reshape(lax.axis_size(axis), -1, width), axis, split_axis=0, concat_axis=0, tiled=True
        )
        part = jnp.sum(pieces.astype(jnp.float32), axis=0).astype(jnp.bfloat16)
    for axis in ("expert", "dp"):
        part = lax.all_gather(part, axis, axis=0, tiled=True)
    small = part[4 * half :].reshape(-1).astype(jnp.float32)
    part = part[: 4 * half].reshape(4, half, width).astype(jnp.float32)

    def own(index, shape):
        return small[edges[index] : edges[index + 1]].reshape(shape)

    shares = (
        own(0, (half,)),
        own(1, (half,)),
        part[0],
        part[1],
        part[2],
        part[3],
        own(2, (half, experts)),
        own(3, (heads // 2, BUCKETS)),
    )
    expert_in_grad = expert_in_sum.astype(jnp.float32)
    expert_out_grad = expert_out_sum.astype(jnp.float32)
    return (
        mixed.astype(jnp.bfloat16),
        grad_tokens,
        shares[0],
        shares[1],
        shares[2],
        shares[3],
        shares[4],
        shares[5],
        shares[6],
        shares[7],
        expert_in_grad,
        expert_out_grad,
    )


def solution(mesh):
    return jax.shard_map(
        per_device,
        mesh=mesh,
        in_specs=(
            P(("dp", "expert", "wshard"), None),
            P(("dp", "expert", "wshard"), None),
            P(("dp", "expert", "wshard"), None),
            P(("dp", "expert", "wshard"), None),
            P("wshard"),
            P("wshard"),
            P("wshard", None),
            P("wshard", None),
            P("wshard", None),
            P("wshard", None),
            P("wshard", None),
            P("wshard", None),
            P(("expert", "wshard"), None, None),
            P(("expert", "wshard"), None, None),
        ),
        out_specs=(
            P(("dp", "expert", "wshard"), None),
            P(("dp", "expert", "wshard"), None),
            P("wshard"),
            P("wshard"),
            P("wshard", None),
            P("wshard", None),
            P("wshard", None),
            P("wshard", None),
            P("wshard", None),
            P("wshard", None),
            P(("expert", "wshard"), None, "dp"),
            P(("expert", "wshard"), "dp", None),
        ),
        check_vma=False,
    )
```

```python
import jax
import jax.numpy as jnp
import numpy as np
from jax import lax
from jax.sharding import PartitionSpec as P

BUCKETS = 32
MAX_DISTANCE = 128


EPS = 1e-06


def bucket_edges():
    half = BUCKETS // 2
    spans = np.arange(half, MAX_DISTANCE)
    levels = half + np.floor(
        np.log(spans / float(half)) / np.log(MAX_DISTANCE / float(half)) * half
    ).astype(np.int64)
    return [
        int(spans[levels >= level][0])
        for level in range(half + 1, BUCKETS)
        if np.any(levels >= level)
    ]


def bucket_of(distance):
    distance = jnp.maximum(distance, 0)
    bucket = jnp.minimum(distance, BUCKETS // 2)
    for edge in bucket_edges():
        bucket = bucket + (distance >= edge).astype(jnp.int32)
    return bucket


def contract(left, right, left_dim, right_dim):
    return lax.dot_general(
        left, right, (((left_dim,), (right_dim,)), ((), ())), preferred_element_type=jnp.float32
    )


def send_rows(rows):
    moved = lax.all_to_all(rows, ("expert", "wshard"), split_axis=0, concat_axis=0, tiled=True)
    return moved


def send_results(rows):
    moved = lax.all_to_all(rows, ("expert", "wshard"), split_axis=0, concat_axis=0, tiled=True)
    return moved


def send_grads(rows):
    moved = lax.all_to_all(rows, ("expert", "wshard"), split_axis=0, concat_axis=0, tiled=True)
    return moved


def send_row_grads(rows):
    moved = lax.all_to_all(rows, ("expert", "wshard"), split_axis=0, concat_axis=0, tiled=True)
    return moved


def block_scores(query_block, key_rows, start, segment, table, block, length, scale):
    rows = start + jnp.arange(block, dtype=jnp.int32)
    distance = rows[:, None] - jnp.arange(length, dtype=jnp.int32)[None, :]
    allowed = (distance >= 0) & (segment[:, None] == segment[None, :])
    onehot = (bucket_of(distance)[..., None] == jnp.arange(BUCKETS, dtype=jnp.int32)).astype(
        jnp.bfloat16
    )
    bias = jnp.einsum("qkb,hb->hqk", onehot, table, preferred_element_type=jnp.float32)
    raw = jnp.einsum("qhd,khd->hqk", query_block, key_rows, preferred_element_type=jnp.float32)
    scores = raw * scale + bias
    return (jnp.where(allowed[None], scores, -1e30), onehot)


def norm_back(grad_normed, inputs, rms, gain):
    unit = inputs * rms
    grad_gain = jnp.sum(grad_normed * unit, axis=0)
    scaled = grad_normed * gain
    return (grad_gain, rms * (scaled - unit * jnp.mean(scaled * unit, axis=-1, keepdims=True)))


def per_device(
    tokens,
    cotangent,
    segment_ids,
    routes,
    gain_attn,
    gain_ffn,
    w_query,
    w_key,
    w_value,
    w_project,
    router,
    bias_table,
    expert_in,
    expert_out,
):
    gathered = (
        lax.all_gather(gain_attn, "wshard", axis=0, tiled=True),
        lax.all_gather(gain_ffn, "wshard", axis=0, tiled=True),
        lax.all_gather(w_query, "wshard", axis=0, tiled=True),
        lax.all_gather(w_key, "wshard", axis=0, tiled=True),
        lax.all_gather(w_value, "wshard", axis=0, tiled=True),
        lax.all_gather(w_project, "wshard", axis=0, tiled=True),
        lax.all_gather(router, "wshard", axis=0, tiled=True),
        lax.all_gather(bias_table, "wshard", axis=0, tiled=True),
    )
    gain_one, gain_two, query_full, key_full, value_full, project_full, router_full, table_full = (
        gathered
    )
    gain_one = gain_one.astype(jnp.float32)
    gain_two = gain_two.astype(jnp.float32)
    length, width = tokens.shape
    heads = table_full.shape[0]
    head_size = width // heads
    experts = router_full.shape[1]
    capacity = 5 * length // (2 * experts)
    block = min(512, length)
    scale = head_size ** (-0.5)
    segment = segment_ids[0]
    starts = jnp.arange(length // block, dtype=jnp.int32) * block
    flat = routes.reshape(-1)
    onehot_int = (flat[:, None] == jnp.arange(experts, dtype=jnp.int32)[None, :]).astype(jnp.int32)
    slot_place = jnp.sum(jnp.cumsum(onehot_int, axis=0) * onehot_int, axis=-1) - 1
    dest = (flat * capacity + slot_place).reshape(length, 2)
    slots = jnp.arange(experts * capacity, dtype=jnp.int32)
    takes_first = slots[:, None] == dest[None, :, 0]
    takes_second = slots[:, None] == dest[None, :, 1]
    spread = (takes_first | takes_second).astype(jnp.bfloat16)
    pick_first = (dest[:, 0][:, None] == slots[None, :]).astype(jnp.bfloat16)
    pick_second = (dest[:, 1][:, None] == slots[None, :]).astype(jnp.bfloat16)

    def to_slots(rows):
        placed = jnp.dot(spread, rows, preferred_element_type=jnp.float32).astype(jnp.bfloat16)
        return placed.reshape(experts, capacity, width)

    cotangent_arrived = send_grads(to_slots(cotangent)).reshape(-1, width)
    inputs = tokens.astype(jnp.float32)
    rms_one = lax.rsqrt(jnp.mean(inputs * inputs, axis=-1, keepdims=True) + EPS)
    normed = (inputs * rms_one * gain_one).astype(jnp.bfloat16)
    joined_weight = jnp.concatenate([query_full, key_full, value_full], axis=1)
    projected = jnp.dot(normed, joined_weight, preferred_element_type=jnp.float32).astype(
        jnp.bfloat16
    )
    queries = projected[:, :width].reshape(length, heads, head_size)
    key_rows = projected[:, width : 2 * width].reshape(length, heads, head_size)
    value_rows = projected[:, 2 * width :].reshape(length, heads, head_size)

    def forward_block(start):
        masked, onehot = block_scores(
            queries, key_rows, start, segment, table_full, block, length, scale
        )
        highest = jnp.max(masked, axis=-1, keepdims=True)
        expo = jnp.exp(masked - highest)
        total = jnp.sum(expo, axis=-1, keepdims=True)
        probs = expo / total
        logsum = highest[..., 0] + jnp.log(total[..., 0])
        result = jnp.einsum(
            "hqk,khd->qhd",
            probs.astype(jnp.bfloat16),
            value_rows,
            preferred_element_type=jnp.float32,
        )
        return (result, logsum)

    attended, logsums = lax.map(forward_block, starts)
    attended = attended.reshape(length, width).astype(jnp.bfloat16)
    branch = jnp.dot(attended, project_full, preferred_element_type=jnp.float32)
    resid = inputs + branch
    rms_two = lax.rsqrt(jnp.mean(resid * resid, axis=-1, keepdims=True) + EPS)
    normed_two = (resid * rms_two * gain_two).astype(jnp.bfloat16)
    logits = jnp.dot(normed_two, router_full, preferred_element_type=jnp.float32)
    chosen_mask = routes[..., None] == jnp.arange(experts, dtype=jnp.int32)
    chosen = jnp.sum(jnp.where(chosen_mask, logits[:, None, :], 0.0), axis=-1)
    gates = jax.nn.softmax(chosen, axis=-1)
    normed_two, cotangent_arrived = lax.optimization_barrier((normed_two, cotangent_arrived))
    arrived = send_rows(to_slots(normed_two))
    gate_slots = jnp.sum(
        jnp.where(takes_first, gates[:, 0][None, :], 0.0)
        + jnp.where(takes_second, gates[:, 1][None, :], 0.0),
        axis=1,
    )
    arrived, gate_slots = lax.optimization_barrier((arrived, gate_slots))
    gate_arrived = send_rows(gate_slots.reshape(experts, capacity)).reshape(-1)
    rows_in = arrived.reshape(-1, width)
    pre = jnp.dot(rows_in, expert_in[0], preferred_element_type=jnp.float32)
    hidden = jax.nn.gelu(pre).astype(jnp.bfloat16)
    produced = jnp.dot(hidden, expert_out[0], preferred_element_type=jnp.float32).astype(
        jnp.bfloat16
    )
    produced, gate_arrived = lax.optimization_barrier((produced, gate_arrived))
    returned = send_results(produced.reshape(experts, capacity, width)).reshape(-1, width)
    grad_arrived = (gate_arrived[:, None] * cotangent_arrived.astype(jnp.float32)).astype(
        jnp.bfloat16
    )
    grad_hidden = contract(grad_arrived, expert_out[0], 1, 1)
    unused, gelu_back = jax.vjp(jax.nn.gelu, pre)
    grad_pre = gelu_back(grad_hidden)[0].astype(jnp.bfloat16)
    returned, grad_pre = lax.optimization_barrier((returned, grad_pre))
    grad_rows = contract(grad_pre, expert_in[0], 1, 1).astype(jnp.bfloat16)
    grad_rows, grad_pre, hidden = lax.optimization_barrier((grad_rows, grad_pre, hidden))
    grad_out_weight = contract(hidden, grad_arrived, 0, 0).astype(jnp.bfloat16)
    grad_in_weight = contract(rows_in, grad_pre, 0, 0).astype(jnp.bfloat16)
    expert_out_sum = lax.psum_scatter(
        grad_out_weight[None], "dp", scatter_dimension=1, tiled=True
    )
    expert_in_sum = lax.psum_scatter(grad_in_weight[None], "dp", scatter_dimension=2, tiled=True)
    grad_back = send_row_grads(grad_rows.reshape(experts, capacity, width)).reshape(-1, width)
    grad_back, unused_out, unused_in = lax.optimization_barrier(
        (grad_back, grad_out_weight, grad_in_weight)
    )
    picked_first = jnp.dot(pick_first, returned, preferred_element_type=jnp.float32)
    picked_second = jnp.dot(pick_second, returned, preferred_element_type=jnp.float32)
    mixed = resid + (gates[:, :1] * picked_first + gates[:, 1:] * picked_second)
    grad_out = cotangent.astype(jnp.float32)
    grad_gates = jnp.stack(
        [jnp.sum(grad_out * picked_first, axis=-1), jnp.sum(grad_out * picked_second, axis=-1)],
        axis=-1,
    )
    grad_normed_two = jnp.dot(
        pick_first + pick_second, grad_back, preferred_element_type=jnp.float32
    )
    grad_chosen = gates * (grad_gates - jnp.sum(gates * grad_gates, axis=-1, keepdims=True))
    grad_logits = jnp.sum(jnp.where(chosen_mask, grad_chosen[..., None], 0.0), axis=1).astype(
        jnp.bfloat16
    )
    grad_router = contract(normed_two, grad_logits, 0, 0)
    grad_normed_two = grad_normed_two + contract(grad_logits, router_full, 1, 1)
    grad_gain_two, grad_resid_norm = norm_back(grad_normed_two, resid, rms_two, gain_two)
    grad_resid = grad_out + grad_resid_norm
    grad_branch = grad_resid.astype(jnp.bfloat16)
    grad_project = contract(attended, grad_branch, 0, 0)
    grad_attended = (
        contract(grad_branch, project_full, 1, 1)
        .astype(jnp.bfloat16)
        .reshape(length, heads, head_size)
    )

    def backward_block(carry, inputs_block):
        grad_keys, grad_values, grad_table = carry
        start, logsum = inputs_block
        masked, onehot = block_scores(
            queries, key_rows, start, segment, table_full, block, length, scale
        )
        probs = jnp.exp(masked - logsum[..., None])
        grad_probs = jnp.einsum(
            "qhd,khd->hqk", grad_attended, value_rows, preferred_element_type=jnp.float32
        )
        inner = jnp.sum(probs * grad_probs, axis=-1, keepdims=True)
        grad_scores = (probs * (grad_probs - inner)).astype(jnp.bfloat16)
        grad_query_block = (
            jnp.einsum("hqk,khd->qhd", grad_scores, key_rows, preferred_element_type=jnp.float32)
            * scale
        )
        grad_keys = (
            grad_keys
            + jnp.einsum("hqk,qhd->khd", grad_scores, queries, preferred_element_type=jnp.float32)
            * scale
        )
        grad_values = grad_values + jnp.einsum(
            "hqk,qhd->khd",
            probs.astype(jnp.bfloat16),
            grad_attended,
            preferred_element_type=jnp.float32,
        )
        grad_table = grad_table + jnp.einsum(
            "hqk,qkb->hb", grad_scores, onehot, preferred_element_type=jnp.float32
        )
        return ((grad_keys, grad_values, grad_table), grad_query_block)

    zero_rows = jnp.zeros((length, heads, head_size), jnp.float32)
    start_carry = (zero_rows, zero_rows, jnp.zeros((heads, BUCKETS), jnp.float32))
    (grad_keys, grad_values, grad_table), grad_queries = lax.scan(
        backward_block, start_carry, (starts, logsums)
    )
    grad_joined = jnp.concatenate(
        [
            grad_queries.reshape(length, width),
            grad_keys.reshape(length, width),
            grad_values.reshape(length, width),
        ],
        axis=1,
    ).astype(jnp.bfloat16)
    grad_weights = contract(normed, grad_joined, 0, 0)
    grad_normed = contract(grad_joined, joined_weight, 1, 1)
    grad_gain_one, grad_input_norm = norm_back(grad_normed, inputs, rms_one, gain_one)
    grad_tokens = grad_resid + grad_input_norm
    half = width // 2
    group = lax.axis_size("dp") * lax.axis_size("expert") * 8
    small = jnp.concatenate(
        [
            grad_gain_one.reshape(2, -1),
            grad_gain_two.reshape(2, -1),
            grad_router.reshape(2, -1),
            grad_table.reshape(2, -1),
        ],
        axis=1,
    ).astype(jnp.bfloat16)
    edges = np.cumsum([0, half, half, half * experts, heads // 2 * BUCKETS])
    extra = -(-int(edges[-1]) // (group * width)) * group
    small = jnp.pad(small, ((0, 0), (0, extra * width - int(edges[-1])))).reshape(2, extra, width)
    large = jnp.stack(
        [
            grad_weights[:, :width],
            grad_weights[:, width : 2 * width],
            grad_weights[:, 2 * width :],
            grad_project,
        ]
    ).astype(jnp.bfloat16)
    large = large.reshape(4, 2, half, width).transpose(1, 0, 2, 3).reshape(2, 4 * half, width)
    large = jnp.concatenate([large, small], axis=1)
    core = lax.axis_index("wshard")
    keep = lax.dynamic_index_in_dim(large, core, 0, keepdims=False)
    give = lax.dynamic_index_in_dim(large, 1 - core, 0, keepdims=False)
    got = lax.ppermute(give, "wshard", [(0, 1), (1, 0)])
    part = (keep.astype(jnp.float32) + got.astype(jnp.float32)).astype(jnp.bfloat16)
    for axis in ("dp", "expert"):
        pieces = lax.all_to_all(
            part.reshape(lax.axis_size(axis), -1, width), axis, split_axis=0, concat_axis=0, tiled=True
        )
        part = jnp.sum(pieces.astype(jnp.float32), axis=0).astype(jnp.bfloat16)
    for axis in ("expert", "dp"):
        part = lax.all_gather(part, axis, axis=0, tiled=True)
    small = part[4 * half :].reshape(-1).astype(jnp.float32)
    part = part[: 4 * half].reshape(4, half, width).astype(jnp.float32)

    def own(index, shape):
        return small[edges[index] : edges[index + 1]].reshape(shape)

    shares = (
        own(0, (half,)),
        own(1, (half,)),
        part[0],
        part[1],
        part[2],
        part[3],
        own(2, (half, experts)),
        own(3, (heads // 2, BUCKETS)),
    )
    expert_in_grad = expert_in_sum.astype(jnp.float32)
    expert_out_grad = expert_out_sum.astype(jnp.float32)
    return (
        mixed.astype(jnp.bfloat16),
        grad_tokens,
        shares[0],
        shares[1],
        shares[2],
        shares[3],
        shares[4],
        shares[5],
        shares[6],
        shares[7],
        expert_in_grad,
        expert_out_grad,
    )


def solution(mesh):
    return jax.shard_map(
        per_device,
        mesh=mesh,
        in_specs=(
            P(("dp", "expert", "wshard"), None),
            P(("dp", "expert", "wshard"), None),
            P(("dp", "expert", "wshard"), None),
            P(("dp", "expert", "wshard"), None),
            P("wshard"),
            P("wshard"),
            P("wshard", None),
            P("wshard", None),
            P("wshard", None),
            P("wshard", None),
            P("wshard", None),
            P("wshard", None),
            P(("expert", "wshard"), None, None),
            P(("expert", "wshard"), None, None),
        ),
        out_specs=(
            P(("dp", "expert", "wshard"), None),
            P(("dp", "expert", "wshard"), None),
            P("wshard"),
            P("wshard"),
            P("wshard", None),
            P("wshard", None),
            P("wshard", None),
            P("wshard", None),
            P("wshard", None),
            P("wshard", None),
            P(("expert", "wshard"), None, "dp"),
            P(("expert", "wshard"), "dp", None),
        ),
        check_vma=False,
    )
```
